128 devices in a mesh: gx: 8 (over z, y_lo), gy: 16 (over y_hi, x, core).
Axes of the slice: x: 4, y: 4 (y_hi: 2, y_lo: 2; y = y_hi * 2 + y_lo), z: 4, core: 2. Of those that a mesh axis runs over, the one named last changes fastest.
Arguments:
- corpus: bfloat16 [262144, 1024], P(('gx', 'gy')), may hold values from -6 to 6
- rotation_first: bfloat16 [16, 1024, 1024], P('gy', 'gx'), may hold values from -0.1875 to 0.1875
- rotation_second: bfloat16 [8, 1024, 1024], P('gx', 'gy'), may hold values from -0.1875 to 0.1875
- cross_first: int32 [8, 16, 1024], P('gx', 'gy'), may hold values from 0 to 2047, as said below
- cross_second: int32 [8, 16, 1024], P('gx', 'gy'), may hold values from 0 to 2047, as said below
Outputs:
- partitioned: bfloat16 [262144, 1024], P(('gx', 'gy'))
The draws below stay inside these ranges and needn't reach their ends.
Inputs may be any that keep to these rules, and one draw needn't show every extreme that they name: For every block, the 1024 entries of cross_first are distinct local row indices. For every block, the 1024 entries of cross_second are distinct local row indices.
All inputs are finite; a program needn't handle non-finite values.
Results may differ from the reference program's by a relative error of at most 0.0049.
Values may be sent and summed in bfloat16 or wider, within the bound.
A program may use at most 64 MiB of HBM per device.

```python
import jax
import jax.numpy as jnp
from jax import lax

D = 1024
ROW_DEV = 2048
ROWS = 262144
N_GX = 8
N_GY = 16


def pick_rows(key):
    key_bits, key_order = jax.random.split(key)
    halves = ROW_DEV // 2
    bits = jax.random.randint(key_bits, (halves,), 0, 2).astype(jnp.int32)
    chosen = 2 * jnp.arange(halves, dtype=jnp.int32) + bits
    order = jax.random.permutation(key_order, halves)
    return chosen[order]


def draw_all(key):
    keys = jax.random.split(key, N_GX * N_GY)
    lists = jax.vmap(pick_rows)(keys)
    return lists.reshape(N_GX, N_GY, ROW_DEV // 2)


def draw_cross_first(key, part):
    return draw_all(jax.random.fold_in(key, 11))


def draw_cross_second(key, part):
    return draw_all(jax.random.fold_in(key, 23))


def block_scale(key, shape, shards, smallest, top_value):
    loudness, own = 1.0, jax.random.fold_in(key, 6)
    for position, shards_of in shards:
        heights = jnp.exp(jax.random.uniform(jax.random.fold_in(own, position), (shards_of,), jnp.float32, smallest / len(shards), top_value / len(shards)))
        loudness = loudness * jnp.repeat(heights, shape[position] // shards_of).reshape([-1 if axis == position else 1 for axis in range(len(shape))])
    return loudness


def scatter_about(own_key, extent, scale, reach, cuts=(), kind=jnp.bfloat16):
    array = scale * jax.random.normal(own_key, extent, jnp.float32)
    if cuts:
        array = array * block_scale(own_key, extent, cuts, -0.22, 0.18)
    return jnp.clip(array, -reach, reach).astype(kind)


def setup_inputs(seed: int = 0) -> dict:
    key_of = jax.random.split(jax.random.key(seed), 6)
    return {
        "corpus": scatter_about(key_of[0], (ROWS, D), 1.0, 6.0, ((0, 128),)),
        "rotation_first": scatter_about(key_of[1], (N_GY, D, D), D ** -0.5, 0.1875, ((0, 16), (1, 8))),
        "rotation_second": scatter_about(key_of[2], (N_GX, D, D), D ** -0.5, 0.1875, ((0, 8), (1, 16))),
        "cross_first": draw_cross_first(jax.random.fold_in(key_of[5], 71), 0),
        "cross_second": draw_cross_second(jax.random.fold_in(key_of[5], 71), 0),
    }


def place_rows(block, index, rows):
    return block.at[index].set(rows)


def cross(data, index, axis):
    sent = jnp.take_along_axis(data, index[..., None], axis=2)
    received = jnp.roll(sent, data.shape[axis] // 2, axis=axis)
    return jax.vmap(jax.vmap(place_rows))(data, index, received)


def reference(corpus, rotation_first, rotation_second, cross_first, cross_second):
    blocks = corpus.reshape(N_GX, N_GY, ROW_DEV, D)
    rot_wide = rotation_first.astype(jnp.float32)

    def first_level(group):
        return jnp.einsum("brd,bde->bre", group.astype(jnp.float32), rot_wide).astype(jnp.bfloat16)

    level_one = lax.map(first_level, blocks)
    moved_one = cross(level_one, cross_first, 0)

    def second_level(pair):
        group, rotation = pair
        flat = group.reshape(N_GY * ROW_DEV, D)
        out = jnp.dot(flat, rotation, preferred_element_type=jnp.float32).astype(jnp.bfloat16)
        return out.reshape(N_GY, ROW_DEV, D)

    level_two = lax.map(second_level, (moved_one, rotation_second))
    partitioned = cross(level_two, cross_second, 1)
    return partitioned.reshape(N_GX * N_GY * ROW_DEV, D)
```

```python
import jax
import jax.numpy as jnp
from jax import lax
from jax.experimental import pallas as pl
from jax.experimental.pallas import tpu as pltpu
from jax.sharding import PartitionSpec as P

MESH = pl.DeviceIdType.MESH
F32, BF16 = jnp.float32, jnp.bfloat16

D = 1024
ROWS = 2048
HALF = 1024
CHUNK = 128
STEPS = HALF // CHUNK
FIRST = 128
SECOND = 64
KEEP = 64
N_FIRST, N_SECOND = 12, 15
BLOCK = 512

AT_SECOND = N_FIRST
AT_ONE = AT_SECOND + N_SECOND
AT_TWO = AT_ONE + STEPS
AT_RANK = AT_TWO + STEPS
FLOWS = AT_RANK + 1


def rows_at(start, size, unit=16):
    if isinstance(start, int):
        return pl.ds(start, size)
    return pl.ds(pl.multiple_of(start, unit), size)


def dot(a, b):
    return jnp.dot(a, b, preferred_element_type=F32)


def ones_where(mask):
    return jnp.where(mask, 1.0, 0.0)


def iota(shape, dim):
    return lax.broadcasted_iota(jnp.int32, shape, dim).astype(F32)


def to_column(row_ref, column_ref):
    same = iota((128, 128), 0) == iota((128, 128), 1)

    @pl.loop(0, HALF // 128)
    def _(b):
        piece = row_ref[0:1, pl.ds(pl.multiple_of(b * 128, 128), 128)]
        column = jnp.sum(jnp.where(same, piece, 0.0), axis=1, keepdims=True)
        column_ref[rows_at(b * 128, 128), :] = jnp.broadcast_to(column, (128, 128))


def over_rows(term):
    def step(b, total):
        return total + jnp.sum(term(b), axis=0, keepdims=True)

    return lax.fori_loop(0, HALF // 128, step, jnp.zeros((1, HALF), F32))


def kernel(
    x_hbm, r1_hbm, r2_hbm, i1_hbm, i2_hbm, out_hbm,
    x, r1, r2, i1, i2, sent1, recv1, held1, raw2, sent2, recv2, y, yr, z, acc,
    col1, col2, colk, colg, rows, rank_out, rank_in,
    send_sem, recv_sem, load_sem, out_sem,
):
    gx, gy = lax.axis_index("gx"), lax.axis_index("gy")
    pz, py = gx // 2, gx % 2
    half, px, pc = gy // 8, (gy // 2) % 4, gy % 2

    def on_z(step):
        return lax.rem(pz + step + 4, 4)

    def part(zz, yy):
        return (zz * 2 + yy) * FIRST

    z_up, z_down, z_far = ((on_z(s) * 2 + py, gy) for s in (1, -1, 2))
    y_near = (pz * 2 + 1 - py, gy)
    far_gy = lax.rem(gy + 8, 16)
    y_far = (gx, far_gy)
    others = [
        (gx, half * 8 + lax.rem(px + dx, 4) * 2 + lax.rem(pc + dc, 2))
        for dx in range(4)
        for dc in range(2)
        if dx or dc
    ]

    loads = [
        pltpu.make_async_copy(src, dst, load_sem.at[i])
        for i, (src, dst) in enumerate(
            (
                (i1_hbm, i1),
                (x_hbm, x),
                (i2_hbm, i2),
                (r1_hbm, r1.at[rows_at(gx * FIRST, FIRST)]),
                (r2_hbm, r2.at[rows_at(gy * SECOND, SECOND)]),
            )
        )
    ]
    for load in loads:
        load.start()

    barrier = pltpu.get_barrier_semaphore()
    partners = [z_up, z_down, z_far, y_near, y_far, *others]
    for partner in partners:
        pl.semaphore_signal(barrier, inc=1, device_id=partner, device_id_type=MESH)
    pl.semaphore_wait(barrier, len(partners))

    def flow(number, src, dst, target):
        return pltpu.make_async_remote_copy(
            src_ref=src,
            dst_ref=dst,
            send_sem=send_sem.at[number],
            recv_sem=recv_sem.at[number],
            device_id=target,
            device_id_type=MESH,
        )

    def first(number, zz, yy, low, size, target, src=None):
        there = r1.at[rows_at(part(zz, yy) + low, size)]
        return flow(number, there if src is None else src, there, target)

    rest = FIRST - KEEP
    f = [
        first(0, pz, py, 0, FIRST, z_up, r1_hbm),
        first(1, pz, py, 0, FIRST, z_down, r1_hbm),
        first(2, pz, py, 0, FIRST, y_near, r1_hbm),
        first(3, on_z(-1), py, 0, 64, z_up),
        first(4, on_z(-1), py, 0, KEEP, y_near),
        first(5, on_z(1), py, 64, 64, z_down),
        first(6, on_z(1), py, 0, KEEP, y_near),
        first(7, pz, 1 - py, KEEP, rest, z_up),
        first(8, pz, 1 - py, KEEP, rest, z_down),
        first(9, on_z(2), py, 0, KEEP, y_near),
        first(10, on_z(-1), 1 - py, KEEP, rest // 2, z_up),
        first(11, on_z(1), 1 - py, KEEP + rest // 2, rest // 2, z_down),
    ]

    def second(number, owner, target, src=None):
        there = r2.at[rows_at(owner * SECOND, SECOND)]
        return flow(AT_SECOND + number, there if src is None else src, there, target)

    s = [second(0, gy, y_far, r2_hbm)]
    s += [second(1 + n, gy, t, r2_hbm) for n, t in enumerate(others)]
    s += [second(8 + n, far_gy, t) for n, t in enumerate(others)]

    def one(c):
        at = rows_at(c * CHUNK, CHUNK)
        return flow(AT_ONE + c, sent1.at[at], recv1.at[at], z_far)

    def two(c):
        at = rows_at(c * CHUNK, CHUNK)
        return flow(AT_TWO + c, sent2.at[at], recv2.at[at], y_far)

    ranks = flow(AT_RANK, rank_out, rank_in, y_far)

    for n in (0, 1, 2):
        f[n].start()
    for n in range(8):
        s[n].start()

    loads[0].wait()
    rows[0:1, :] = i1[...].astype(F32)
    to_column(rows.at[0:1], col1)
    loads[1].wait()

    def pick_one(c):
        at = rows_at(c * CHUNK, CHUNK)
        hot = ones_where(col1[at, 0:1] == iota((CHUNK, ROWS), 1)).astype(BF16)
        sent1[at, :] = dot(hot, x[...]).astype(BF16)

    @pl.loop(0, 2)
    def _(c):
        pick_one(c)
        one(c).start()

    @pl.loop(2, STEPS)
    def _(c):
        pick_one(c)

    f[0].wait_recv()
    f[3].start()
    f[4].start()
    f[1].wait_recv()
    f[5].start()
    f[6].start()
    f[2].wait_recv()
    f[7].start()
    f[8].start()
    one(2).start()
    s[0].wait_recv()
    for n in range(8, 15):
        s[n].start()

    loads[2].wait()
    rows[1:2, :] = i2[...].astype(F32)
    to_column(rows.at[1:2], col2)
    held1[...] = jnp.zeros_like(held1)
    lane = iota((1, HALF), 1)

    def of_block(ref, b):
        return ref[rows_at(b * 128, 128), 0:1]

    own2 = rows[1:2, :]
    key = over_rows(
        lambda b: jnp.where(
            of_block(col1, b) == own2,
            iota((128, HALF), 0) + (b * 128 + 1).astype(F32),
            0.0,
        )
    )
    order = key * HALF + lane
    rows[2:3, :] = order
    to_column(rows.at[2:3], colk)
    rank = over_rows(lambda b: ones_where(of_block(colk, b) < order))
    rank_out[...] = jnp.broadcast_to(rank, rank_out.shape)
    ranks.start()

    f[3].wait_recv()
    f[9].start()
    f[7].wait_recv()
    f[10].start()
    f[8].wait_recv()
    f[11].start()
    for c in range(3, STEPS):
        one(c).start()

    source = jnp.where(key > 0.0, key + (ROWS - 1.0), own2)
    rows[3:4, :] = rank
    rows[4:5, :] = source

    @pl.loop(0, HALF // 128)
    def _(b):
        here = iota((128, HALF), 0) + (b * 128).astype(F32)
        found = jnp.where(rows[3:4, :] == here, rows[4:5, :], 0.0)
        colg[rows_at(b * 128, 128), :] = jnp.broadcast_to(
            jnp.sum(found, axis=1, keepdims=True), (128, 128)
        )

    @pl.loop(0, HALF // 256)
    def _(b):
        at = rows_at(b * 256, 256)
        hot = ones_where(colg[at, 0:1] == iota((256, ROWS), 1)).astype(BF16)
        raw2[at, :] = dot(hot, x[...]).astype(BF16)

    loads[3].wait()
    for n in (4, 5, 6, 9, 10, 11):
        f[n].wait_recv()

    def settle(p):
        at = rows_at(p * CHUNK, CHUNK)
        z[0:CHUNK, :] = dot(yr[at, :], r2[...]).astype(BF16)
        two(p).wait_recv()
        z[CHUNK : 2 * CHUNK, :] = dot(recv2[at, :], r2[...]).astype(BF16)
        lanes = pl.ds(pl.multiple_of(p * CHUNK, CHUNK), CHUNK)
        return jnp.concatenate([rows[5:6, lanes], rows[6:7, lanes]], axis=1)

    def place(to, t):
        at = rows_at(t * BLOCK, BLOCK)
        hit = to == iota((BLOCK, 2 * CHUNK), 0) + (t * BLOCK).astype(F32)
        hot = ones_where(hit)
        new = dot(hot.astype(BF16), z[...])
        old = acc[at, :].astype(F32)
        some = jnp.max(hot, axis=1, keepdims=True)
        acc[at, :] = jnp.where(some > 0.0, new, old).astype(BF16)

    def rotate(src, by, dst, low, high):
        @pl.loop(low, high)
        def _(t):
            at = rows_at(t * BLOCK, BLOCK)
            dst[at, :] = dot(src[at, :], by[...]).astype(BF16)

    @pl.loop(0, STEPS)
    def _(c):
        at = rows_at(c * CHUNK, CHUNK)
        one(c).wait_recv()
        held1[at, :] = recv1[at, :]
        hot = ones_where(colg[at, 0:1] - float(ROWS) == iota((CHUNK, HALF), 1))
        raw = raw2[at, :].astype(F32) + dot(hot.astype(BF16), held1[...])
        sent2[at, :] = dot(raw.astype(BF16), r1[...]).astype(BF16)
        two(c).start()
        yr[at, :] = dot(recv1[at, :], r1[...]).astype(BF16)

        @pl.when(c == 0)
        def _():
            rotate(x, r1, y, 0, 2)
            own1 = rows[0:1, :]
            taken = over_rows(lambda b: ones_where(of_block(col2, b) == own1))
            rows[5:6, :] = jnp.where(taken > 0.0, -1.0, own1)

        @pl.when(c == 1)
        def _():
            rotate(x, r1, y, 2, 4)
            ranks.wait_recv()
            rows[2:3, :] = rank_in[0:1, :]
            to_column(rows.at[2:3], colk)
            lanes = iota((128, HALF), 1)
            rows[6:7, :] = over_rows(
                lambda b: jnp.where(
                    of_block(colk, b) == lanes, of_block(col2, b), 0.0
                )
            )

        @pl.when(c == 2)
        def _():
            loads[4].wait()
            for n in range(1, 15):
                s[n].wait_recv()
            rotate(y, r2, acc, 0, 3)

        @pl.when(c == 3)
        def _():
            rotate(y, r2, acc, 3, 4)

        def since(k):
            return (c >= k).astype(jnp.int32)

        low = since(4) + 2 * since(5) + 2 * since(6) + since(7)
        high = since(3) + 2 * since(4) + 2 * since(5) + since(6) + since(7)

        @pl.loop(low, high)
        def _(p):
            to = settle(p)

            @pl.loop(0, ROWS // BLOCK)
            def _(t):
                place(to, t)

    def write(t):
        at = rows_at(t * BLOCK, BLOCK)
        return pltpu.make_async_copy(acc.at[at], out_hbm.at[at], out_sem.at[t])

    last = settle(STEPS - 1)

    @pl.loop(0, ROWS // BLOCK)
    def _(t):
        place(last, t)
        write(t).start()

    for n in range(N_FIRST):
        f[n].wait_send()
    for n in range(N_SECOND):
        s[n].wait_send()
    ranks.wait_send()
    for c in range(STEPS):
        one(c).wait_send()
        two(c).wait_send()
    for t in range(ROWS // BLOCK):
        write(t).wait()


def on_device(corpus, rotation_first, rotation_second, cross_first, cross_second):
    anywhere = pl.BlockSpec(memory_space=pl.ANY)
    return pl.pallas_call(
        kernel,
        out_shape=jax.ShapeDtypeStruct((ROWS, D), BF16),
        in_specs=[anywhere] * 5,
        out_specs=anywhere,
        scratch_shapes=[
            pltpu.VMEM((ROWS, D), BF16),
            pltpu.VMEM((D, D), BF16),
            pltpu.VMEM((D, D), BF16),
            pltpu.VMEM((1, HALF), jnp.int32),
            pltpu.VMEM((1, HALF), jnp.int32),
            pltpu.VMEM((HALF, D), BF16),
            pltpu.VMEM((HALF, D), BF16),
            pltpu.VMEM((HALF, D), BF16),
            pltpu.VMEM((HALF, D), BF16),
            pltpu.VMEM((HALF, D), BF16),
            pltpu.VMEM((HALF, D), BF16),
            pltpu.VMEM((ROWS, D), BF16),
            pltpu.VMEM((HALF, D), BF16),
            pltpu.VMEM((2 * CHUNK, D), BF16),
            pltpu.VMEM((ROWS, D), BF16),
            pltpu.VMEM((HALF, 128), F32),
            pltpu.VMEM((HALF, 128), F32),
            pltpu.VMEM((HALF, 128), F32),
            pltpu.VMEM((HALF, 128), F32),
            pltpu.VMEM((8, HALF), F32),
            pltpu.VMEM((8, HALF), F32),
            pltpu.VMEM((8, HALF), F32),
            pltpu.SemaphoreType.DMA((FLOWS,)),
            pltpu.SemaphoreType.DMA((FLOWS,)),
            pltpu.SemaphoreType.DMA((5,)),
            pltpu.SemaphoreType.DMA((ROWS // BLOCK,)),
        ],
        compiler_params=pltpu.CompilerParams(
            collective_id=0, has_side_effects=True, vmem_limit_bytes=48 << 20
        ),
        cost_estimate=pl.CostEstimate(
            flops=36 << 30, bytes_accessed=16 << 20, transcendentals=0
        ),
    )(
        corpus,
        rotation_first.reshape(FIRST, D),
        rotation_second.reshape(SECOND, D),
        cross_first.reshape(1, HALF),
        cross_second.reshape(1, HALF),
    )


def solution(mesh):
    in_specs = (
        P(("gx", "gy"), None),
        P("gy", "gx", None),
        P("gx", "gy", None),
        P("gx", "gy", None),
        P("gx", "gy", None),
    )
    out_specs = P(("gx", "gy"), None)
    return jax.shard_map(
        on_device, mesh=mesh, in_specs=in_specs, out_specs=out_specs, check_vma=False
    )
```

```python
import jax
import jax.numpy as jnp
from jax import lax
from jax.experimental import pallas as pl
from jax.experimental.pallas import tpu as pltpu
from jax.sharding import PartitionSpec as P

MESH = pl.DeviceIdType.MESH
F32, BF16 = jnp.float32, jnp.bfloat16

D = 1024
ROWS = 2048
HALF = 1024
CHUNK = 128
STEPS = HALF // CHUNK
FIRST = 128
SECOND = 64
N_FIRST, N_SECOND = 15, 15
BLOCK = 512
VMEM = 48 << 20
TAIL = 256

AT_SECOND = N_FIRST
AT_ONE = AT_SECOND + N_SECOND
AT_TWO = AT_ONE + STEPS + 1
AT_RANK = AT_TWO + STEPS + 1
FLOWS = AT_RANK + 1


def rows_at(start, size, unit=16):
    if isinstance(start, int):
        return pl.ds(start, size)
    return pl.ds(pl.multiple_of(start, unit), size)


def dot(a, b):
    return jnp.dot(a, b, preferred_element_type=F32)


def ones_where(mask):
    return jnp.where(mask, 1.0, 0.0)


def iota(shape, dim):
    return lax.broadcasted_iota(jnp.int32, shape, dim).astype(F32)


def to_column(row_ref, column_ref):
    same = iota((128, 128), 0) == iota((128, 128), 1)

    @pl.loop(0, HALF // 128)
    def _(b):
        piece = row_ref[0:1, pl.ds(pl.multiple_of(b * 128, 128), 128)]
        column = jnp.sum(jnp.where(same, piece, 0.0), axis=1, keepdims=True)
        column_ref[rows_at(b * 128, 128), :] = jnp.broadcast_to(column, (128, 128))


def over_rows(term):
    def step(b, total):
        return total + jnp.sum(term(b), axis=0, keepdims=True)

    return lax.fori_loop(0, HALF // 128, step, jnp.zeros((1, HALF), F32))


def kernel(
    x_hbm, r1_hbm, r2_hbm, i1_hbm, i2_hbm, acc, last_ref, to_ref,
    x, r1, r2, i1, i2, sent1, recv1, held1, raw2, sent2, y, late, z,
    col1, col2, colk, colg, keep, count, rows, to, rank_out, rank_in,
    send_sem, recv_sem, load_sem,
):
    gx, gy = lax.axis_index("gx"), lax.axis_index("gy")
    pz, py = gx // 2, gx % 2
    half, px, pc = gy // 8, (gy // 2) % 4, gy % 2

    def on_z(step):
        return lax.rem(pz + step + 4, 4)

    def part(zz, yy):
        return (zz * 2 + yy) * FIRST

    z_up, z_down, z_far = ((on_z(s) * 2 + py, gy) for s in (1, -1, 2))
    y_near = (pz * 2 + 1 - py, gy)
    far_gy = lax.rem(gy + 8, 16)
    y_far = (gx, far_gy)
    others = [
        (gx, half * 8 + lax.rem(px + dx, 4) * 2 + lax.rem(pc + dc, 2))
        for dx in range(4)
        for dc in range(2)
        if dx or dc
    ]

    loads = [
        pltpu.make_async_copy(src, dst, load_sem.at[i])
        for i, (src, dst) in enumerate(
            (
                (i1_hbm.at[0], i1),
                (i2_hbm.at[0], i2),
                (x_hbm, x),
                (r1_hbm.at[0], r1.at[rows_at(gx * FIRST, FIRST)]),
                (r2_hbm.at[0], r2.at[rows_at(gy * SECOND, SECOND)]),
            )
        )
    ]
    for load in loads:
        load.start()

    barrier = pltpu.get_barrier_semaphore()
    partners = [z_up, z_down, z_far, y_near, y_far, *others]
    for partner in partners:
        pl.semaphore_signal(barrier, inc=1, device_id=partner, device_id_type=MESH)
    pl.semaphore_wait(barrier, len(partners))

    def flow(number, src, dst, target):
        return pltpu.make_async_remote_copy(
            src_ref=src,
            dst_ref=dst,
            send_sem=send_sem.at[number],
            recv_sem=recv_sem.at[number],
            device_id=target,
            device_id_type=MESH,
        )

    def first(number, zz, yy, low, size, target, src=None):
        there = r1.at[rows_at(part(zz, yy) + low, size)]
        return flow(number, there if src is None else src, there, target)

    low, high = 0, FIRST // 2
    f = {
        "up_low": first(0, pz, py, low, 64, z_up, r1_hbm.at[0, 0:64]),
        "down_high": first(1, pz, py, high, 64, z_down, r1_hbm.at[0, 64:128]),
        "near_high": first(2, pz, py, high, 64, y_near, r1_hbm.at[0, 64:128]),
        "up_high": first(3, pz, py, high, 64, z_up, r1_hbm.at[0, 64:128]),
        "down_low": first(4, pz, py, low, 64, z_down, r1_hbm.at[0, 0:64]),
        "near_low": first(5, pz, py, low, 64, y_near, r1_hbm.at[0, 0:64]),
        "up_low_2": first(6, on_z(-1), py, low, 64, z_up),
        "down_high_2": first(7, on_z(1), py, high, 64, z_down),
        "near_up": first(8, on_z(-1), py, low, 64, y_near),
        "near_down": first(9, on_z(1), py, low, 64, y_near),
        "up_near": first(10, pz, 1 - py, high, 64, z_up),
        "down_near": first(11, pz, 1 - py, high, 64, z_down),
        "near_far": first(12, on_z(2), py, low, 64, y_near),
        "up_near_2": first(13, on_z(-1), 1 - py, high, 32, z_up),
        "down_near_2": first(14, on_z(1), 1 - py, high + 32, 32, z_down),
    }

    def forward(came, *names):
        f[came].wait_recv()
        for name in names:
            f[name].start()

    def second(number, owner, target, src=None):
        there = r2.at[rows_at(owner * SECOND, SECOND)]
        return flow(AT_SECOND + number, there if src is None else src, there, target)

    s = [second(0, gy, y_far, r2_hbm.at[0])]
    s += [second(1 + n, gy, t, r2_hbm.at[0]) for n, t in enumerate(others)]
    s += [second(8 + n, far_gy, t) for n, t in enumerate(others)]

    def one(c, at=0, size=CHUNK, number=None):
        rows_of = rows_at(c * CHUNK + at, size)
        number = c if number is None else number
        return flow(AT_ONE + number, sent1.at[rows_of], recv1.at[rows_of], z_far)

    def two(c, at=0, size=CHUNK, number=None):
        source = sent2.at[rows_at(c * CHUNK + at, size)]
        target = late.at[rows_at(c * 2 * CHUNK + CHUNK + at, size)]
        number = c if number is None else number
        return flow(AT_TWO + number, source, target, y_far)

    small = CHUNK // 2
    one_halves = [one(0, h * small, small, h * STEPS) for h in range(2)]
    two_halves = [two(0, h * small, small, h * STEPS) for h in range(2)]

    ranks = flow(AT_RANK, rank_out, rank_in, y_far)

    for name in list(f)[:6]:
        f[name].start()
    for n in range(1, 8):
        s[n].start()

    lane = iota((1, HALF), 1)

    def of_block(ref, b):
        return ref[rows_at(b * 128, 128), 0:1]

    loads[0].wait()
    rows[0:1, :] = i1[...].astype(F32)
    to_column(rows.at[0:1], col1)
    loads[1].wait()
    rows[1:2, :] = i2[...].astype(F32)
    own2 = rows[1:2, :]
    key = over_rows(
        lambda b: jnp.where(
            of_block(col1, b) == own2,
            iota((128, HALF), 0) + (b * 128 + 1).astype(F32),
            0.0,
        )
    )
    order = key * HALF + lane
    rows[2:3, :] = order
    rows[4:5, :] = jnp.where(key > 0.0, key + (ROWS - 1.0), own2)
    to_column(rows.at[2:3], colk)

    forward("up_low", "up_low_2", "near_up")
    forward("down_high", "down_high_2")
    forward("near_high", "up_near", "down_near")
    forward("down_low", "near_down")
    s[0].start()

    loads[2].wait()

    def pick_one(c):
        at = rows_at(c * 2 * CHUNK, 2 * CHUNK)
        hot = ones_where(col1[at, 0:1] == iota((2 * CHUNK, ROWS), 1)).astype(BF16)
        sent1[at, :] = dot(hot, x[...]).astype(BF16)

    pl.loop(0, STEPS // 2)(pick_one)

    forward("up_low_2", "near_far")
    forward("up_near", "up_near_2")
    forward("down_near", "down_near_2")
    s[0].wait_recv()
    for n in range(8, 15):
        s[n].start()

    order = rows[2:3, :]
    rank = over_rows(lambda b: ones_where(of_block(colk, b) < order))
    rank_out[...] = jnp.broadcast_to(rank, rank_out.shape)
    rows[3:4, :] = rank
    ranks.start()
    for name in ("up_high", "down_high_2", "up_near_2", "down_near_2"):
        f[name].wait_recv()
    for half_chunk in one_halves:
        half_chunk.start()
    for c in (1, 2):
        one(c).start()

    @pl.loop(0, HALF // 128)
    def _(b):
        here = iota((128, HALF), 0) + (b * 128).astype(F32)
        found = jnp.where(rows[3:4, :] == here, rows[4:5, :], 0.0)
        colg[rows_at(b * 128, 128), :] = jnp.broadcast_to(
            jnp.sum(found, axis=1, keepdims=True), (128, 128)
        )

    @pl.loop(0, HALF // 256)
    def _(b):
        at = rows_at(b * 256, 256)
        hot = ones_where(colg[at, 0:1] == iota((256, ROWS), 1)).astype(BF16)
        raw2[at, :] = dot(hot, x[...]).astype(BF16)

    held1[...] = jnp.zeros_like(held1)
    to_column(rows.at[1:2], col2)

    def table(ref, column):
        high = jnp.floor(ref * (1 / 128))
        low = column - jnp.floor(column * (1 / 128)) * 128
        hot_high = ones_where(high == iota((ROWS // 128, HALF), 0)).astype(BF16)
        hot_low = ones_where(low == iota((HALF, 128), 1)).astype(BF16)
        return dot(hot_high, hot_low)

    count[...] = table(rows[0:1, :], col1[...]) + table(rows[1:2, :], col2[...])
    same = iota((128, 128), 0) == iota((128, 128), 1)

    @pl.loop(0, ROWS // 128)
    def _(b):
        found = jnp.sum(
            jnp.where(same, count[pl.ds(b, 1), :], 0.0), axis=1, keepdims=True
        )
        column = jnp.where(found > 0.0, 0.0, 1.0)
        keep[rows_at(b * 128, 128), :] = jnp.broadcast_to(column, (128, 128))

    loads[3].wait()
    for name in ("near_low", "near_up", "near_down", "near_far"):
        f[name].wait_recv()

    def place(low, high):
        size = (high - low) * CHUNK
        source = z[low * CHUNK : high * CHUNK, :]
        target = to[0:1, low * CHUNK : high * CHUNK]

        def step(t):
            at = rows_at(t * BLOCK, BLOCK)
            hit = target == iota((BLOCK, size), 0) + (t * BLOCK).astype(F32)
            new = dot(ones_where(hit).astype(BF16), source)
            acc[at, :] = (acc[at, :].astype(F32) + new).astype(BF16)

        return step

    def rotate_block(src, by, dst, t, size=BLOCK):
        at = rows_at(t * size, size)
        dst[at, :] = dot(src[at, :], by[...]).astype(BF16)

    def settle_block(t):
        at = rows_at(t * BLOCK, BLOCK)
        kept = dot(y[at, :], r2[...]) * keep[at, 0:1]
        acc[at, :] = kept.astype(BF16)

    def rotate_came(t):
        came = dot(recv1[rows_at(t * 256, 256), :], r1[...]).astype(BF16)
        late[rows_at(t * 512, CHUNK), :] = came[0:CHUNK, :]
        late[rows_at(t * 512 + 2 * CHUNK, CHUNK), :] = came[CHUNK:, :]

    def pass_on(at):
        held1[at, :] = recv1[at, :]
        size = held1[at, :].shape[0]
        hot = ones_where(colg[at, 0:1] - float(ROWS) == iota((size, HALF), 1))
        raw = raw2[at, :].astype(F32) + dot(hot.astype(BF16), held1[...])
        sent2[at, :] = dot(raw.astype(BF16), r1[...]).astype(BF16)

    for h in range(2):
        one_halves[h].wait_recv()
        if h == 1:
            one(3).start()
        pass_on(pl.ds(h * small, small))
        two_halves[h].start()

    def spread(row, first):
        for p in range(STEPS):
            start = p * 2 * CHUNK + first
            to[0:1, start : start + CHUNK] = row[:, p * CHUNK : (p + 1) * CHUNK]

    def rest(c):
        def at_step(k):
            if isinstance(c, int):
                return lambda work: work() if c == k else None
            return pl.when(c == k) if k else lambda work: None

        @at_step(0)
        def _():
            pl.loop(0, 2)(lambda t: rotate_block(x, r1, y, t))
            own1 = rows[0:1, :]
            taken = over_rows(lambda b: ones_where(of_block(col2, b) == own1))
            spread(jnp.where(taken > 0.0, -1.0, own1), 0)

        @at_step(1)
        def _():
            pl.loop(2, 4)(lambda t: rotate_block(x, r1, y, t))
            ranks.wait_recv()
            rows[2:3, :] = rank_in[0:1, :]
            to_column(rows.at[2:3], colk)
            lanes = iota((128, HALF), 1)
            spread(
                over_rows(
                    lambda b: jnp.where(
                        of_block(colk, b) == lanes, of_block(col2, b), 0.0
                    )
                ),
                CHUNK,
            )

        @at_step(2)
        def _():
            loads[4].wait()
            for n in range(1, 15):
                s[n].wait_recv()
            pl.loop(0, 3)(settle_block)

        @at_step(3)
        def _():
            settle_block(jnp.int32(3))
            pl.loop(0, 2)(rotate_came)

        @at_step(4)
        def _():
            for half_chunk in two_halves:
                half_chunk.wait_recv()
            for n in (1, 2, 3):
                two(n).wait_recv()
            pl.loop(0, 2)(lambda t: rotate_block(late, r2, z, t))
            pl.loop(0, 1)(place(0, 8))

        @at_step(5)
        def _():
            pl.loop(1, 4)(place(0, 8))
            rotate_came(jnp.int32(2))

        @at_step(6)
        def _():
            for n in (4, 5):
                two(n).wait_recv()
            rotate_block(late, r2, z, jnp.int32(2))
            pl.loop(0, 4)(place(8, 12))

        @at_step(7)
        def _():
            rotate_came(jnp.int32(3))
            z[14 * CHUNK : 15 * CHUNK, :] = dot(
                late[14 * CHUNK : 15 * CHUNK, :], r2[...]
            ).astype(BF16)
            two(6).wait_recv()
            rotate_block(late, r2, z, jnp.int32(6), 256)
            pl.loop(0, 4)(place(12, 15))

    rest(0)

    @pl.loop(1, STEPS)
    def _(c):
        one(c).wait_recv()

        @pl.when(c < STEPS - 3)
        def _():
            one(c + 3).start()

        pass_on(rows_at(c * CHUNK, CHUNK))
        two(c).start()
        rest(c)

    to_ref[...] = jnp.broadcast_to(to[0:1, 15 * CHUNK :], to_ref.shape)
    two(STEPS - 1).wait_recv()
    last_ref[...] = dot(late[15 * CHUNK :, :], r2[...]).astype(BF16)

    for name in f:
        f[name].wait_send()
    for n in range(N_SECOND):
        s[n].wait_send()
    ranks.wait_send()
    for half_chunk in (*one_halves, *two_halves):
        half_chunk.wait_send()
    for c in range(1, STEPS):
        one(c).wait_send()
        two(c).wait_send()


def finish(acc, last, to, out_ref):
    start = pl.program_id(0) * TAIL
    hot = ones_where(to[0:1, :] == iota((TAIL, CHUNK), 0) + start.astype(F32))
    new = dot(hot.astype(BF16), last[...])
    old = acc[rows_at(start, TAIL), :].astype(F32)
    out_ref[...] = (old + new).astype(BF16)


def on_device(corpus, rotation_first, rotation_second, cross_first, cross_second):
    hbm = pl.BlockSpec(memory_space=pltpu.HBM)
    vmem = pl.BlockSpec(memory_space=pltpu.VMEM)
    acc, last, to = pl.pallas_call(
        kernel,
        out_shape=(
            jax.ShapeDtypeStruct((ROWS, D), BF16),
            jax.ShapeDtypeStruct((CHUNK, D), BF16),
            jax.ShapeDtypeStruct((8, CHUNK), F32),
        ),
        in_specs=[hbm] * 5,
        out_specs=(vmem, vmem, vmem),
        scratch_shapes=[
            pltpu.VMEM((ROWS, D), BF16),
            pltpu.VMEM((D, D), BF16),
            pltpu.VMEM((D, D), BF16),
            pltpu.VMEM((1, HALF), jnp.int32),
            pltpu.VMEM((1, HALF), jnp.int32),
            pltpu.VMEM((HALF, D), BF16),
            pltpu.VMEM((HALF, D), BF16),
            pltpu.VMEM((HALF, D), BF16),
            pltpu.VMEM((HALF, D), BF16),
            pltpu.VMEM((HALF, D), BF16),
            pltpu.VMEM((ROWS, D), BF16),
            pltpu.VMEM((ROWS, D), BF16),
            pltpu.VMEM((ROWS, D), BF16),
            pltpu.VMEM((HALF, 128), F32),
            pltpu.VMEM((HALF, 128), F32),
            pltpu.VMEM((HALF, 128), F32),
            pltpu.VMEM((HALF, 128), F32),
            pltpu.VMEM((ROWS, 128), F32),
            pltpu.VMEM((ROWS // 128, 128), F32),
            pltpu.VMEM((8, HALF), F32),
            pltpu.VMEM((8, ROWS), F32),
            pltpu.VMEM((8, HALF), F32),
            pltpu.VMEM((8, HALF), F32),
            pltpu.SemaphoreType.DMA((FLOWS,)),
            pltpu.SemaphoreType.DMA((FLOWS,)),
            pltpu.SemaphoreType.DMA((5,)),
        ],
        compiler_params=pltpu.CompilerParams(
            collective_id=0, has_side_effects=True, vmem_limit_bytes=VMEM
        ),
        cost_estimate=pl.CostEstimate(
            flops=36_000_000_000, bytes_accessed=16 << 20, transcendentals=0
        ),
    )(
        corpus,
        rotation_first,
        rotation_second,
        cross_first,
        cross_second,
    )
    return pl.pallas_call(
        finish,
        grid=(ROWS // TAIL,),
        out_shape=jax.ShapeDtypeStruct((ROWS, D), BF16),
        in_specs=[vmem] * 3,
        out_specs=pl.BlockSpec((TAIL, D), lambda t: (t, 0)),
        compiler_params=pltpu.CompilerParams(vmem_limit_bytes=12 << 20),
        cost_estimate=pl.CostEstimate(
            flops=600_000_000, bytes_accessed=8 << 20, transcendentals=0
        ),
    )(acc, last, to)


def solution(mesh):
    in_specs = (
        P(("gx", "gy"), None),
        P("gy", "gx", None),
        P("gx", "gy", None),
        P("gx", "gy", None),
        P("gx", "gy", None),
    )
    out_specs = P(("gx", "gy"), None)
    return jax.shard_map(
        on_device, mesh=mesh, in_specs=in_specs, out_specs=out_specs, check_vma=False
    )
```

```python
import jax
import jax.numpy as jnp
from jax import lax
from jax.experimental import pallas as pl
from jax.experimental.pallas import tpu as pltpu
from jax.sharding import PartitionSpec as P

MESH = pl.DeviceIdType.MESH
F32, BF16 = jnp.float32, jnp.bfloat16

D = 1024
ROWS = 2048
HALF = 1024
CHUNK = 128
SMALL = 128
STEPS = HALF // SMALL
AHEAD = 3
FIRST = 128
SECOND = 64
N_FIRST, N_SECOND = 15, 15
BLOCK = 512
VMEM = 48 << 20
TAIL = 256

AT_SECOND = N_FIRST
AT_ONE = AT_SECOND + N_SECOND
AT_TWO = AT_ONE + STEPS
AT_RANK = AT_TWO + STEPS
FLOWS = AT_RANK + 1


def rows_at(start, size, unit=16):
    if isinstance(start, int):
        return pl.ds(start, size)
    return pl.ds(pl.multiple_of(start, unit), size)


def dot(a, b):
    return jnp.dot(a, b, preferred_element_type=F32)


def ones_where(mask):
    return jnp.where(mask, 1.0, 0.0)


def iota(shape, dim):
    return lax.broadcasted_iota(jnp.int32, shape, dim).astype(F32)


def to_column(row_ref, column_ref):
    same = iota((128, 128), 0) == iota((128, 128), 1)

    @pl.loop(0, HALF // 128)
    def _(b):
        piece = row_ref[0:1, pl.ds(pl.multiple_of(b * 128, 128), 128)]
        column = jnp.sum(jnp.where(same, piece, 0.0), axis=1, keepdims=True)
        column_ref[rows_at(b * 128, 128), :] = jnp.broadcast_to(column, (128, 128))


def over_rows(term):
    def step(b, total):
        return total + jnp.sum(term(b), axis=0, keepdims=True)

    return lax.fori_loop(0, HALF // 128, step, jnp.zeros((1, HALF), F32))


def kernel(
    x_hbm, r1_hbm, r2_hbm, i1_hbm, i2_hbm, acc, last_ref, to_ref,
    x, r1, r2, i1, i2, sent1, recv1, held1, raw2, sent2, y, late, z,
    col1, col2, colk, colg, keep, count, rows, to, rank_out, rank_in,
    send_sem, recv_sem, load_sem,
):
    gx, gy = lax.axis_index("gx"), lax.axis_index("gy")
    pz, py = gx // 2, gx % 2
    half, px, pc = gy // 8, (gy // 2) % 4, gy % 2

    def on_z(step):
        return lax.rem(pz + step + 4, 4)

    def part(zz, yy):
        return (zz * 2 + yy) * FIRST

    z_up, z_down, z_far = ((on_z(s) * 2 + py, gy) for s in (1, -1, 2))
    y_near = (pz * 2 + 1 - py, gy)
    far_gy = lax.rem(gy + 8, 16)
    y_far = (gx, far_gy)
    others = [
        (gx, half * 8 + lax.rem(px + dx, 4) * 2 + lax.rem(pc + dc, 2))
        for dx in range(4)
        for dc in range(2)
        if dx or dc
    ]

    loads = [
        pltpu.make_async_copy(src, dst, load_sem.at[i])
        for i, (src, dst) in enumerate(
            (
                (i1_hbm.at[0], i1),
                (i2_hbm.at[0], i2),
                (x_hbm, x),
                (r1_hbm.at[0], r1.at[rows_at(gx * FIRST, FIRST)]),
                (r2_hbm.at[0], r2.at[rows_at(gy * SECOND, SECOND)]),
            )
        )
    ]
    for load in loads:
        load.start()

    barrier = pltpu.get_barrier_semaphore()
    partners = [z_up, z_down, z_far, y_near, y_far, *others]
    for partner in partners:
        pl.semaphore_signal(barrier, inc=1, device_id=partner, device_id_type=MESH)
    pl.semaphore_wait(barrier, len(partners))

    def flow(number, src, dst, target):
        return pltpu.make_async_remote_copy(
            src_ref=src,
            dst_ref=dst,
            send_sem=send_sem.at[number],
            recv_sem=recv_sem.at[number],
            device_id=target,
            device_id_type=MESH,
        )

    def first(number, zz, yy, low, size, target, src=None):
        there = r1.at[rows_at(part(zz, yy) + low, size)]
        return flow(number, there if src is None else src, there, target)

    low, high = 0, FIRST // 2
    f = {
        "up_low": first(0, pz, py, low, 64, z_up, r1_hbm.at[0, 0:64]),
        "down_high": first(1, pz, py, high, 64, z_down, r1_hbm.at[0, 64:128]),
        "near_high": first(2, pz, py, high, 64, y_near, r1_hbm.at[0, 64:128]),
        "up_high": first(3, pz, py, high, 64, z_up, r1_hbm.at[0, 64:128]),
        "down_low": first(4, pz, py, low, 64, z_down, r1_hbm.at[0, 0:64]),
        "near_low": first(5, pz, py, low, 64, y_near, r1_hbm.at[0, 0:64]),
        "up_low_2": first(6, on_z(-1), py, low, 64, z_up),
        "down_high_2": first(7, on_z(1), py, high, 64, z_down),
        "near_up": first(8, on_z(-1), py, low, 64, y_near),
        "near_down": first(9, on_z(1), py, low, 64, y_near),
        "up_near": first(10, pz, 1 - py, high, 64, z_up),
        "down_near": first(11, pz, 1 - py, high, 64, z_down),
        "near_far": first(12, on_z(2), py, low, 64, y_near),
        "up_near_2": first(13, on_z(-1), 1 - py, high, 32, z_up),
        "down_near_2": first(14, on_z(1), 1 - py, high + 32, 32, z_down),
    }

    def forward(came, *names):
        f[came].wait_recv()
        for name in names:
            f[name].start()

    def second(number, owner, target, src=None):
        there = r2.at[rows_at(owner * SECOND, SECOND)]
        return flow(AT_SECOND + number, there if src is None else src, there, target)

    s = [second(0, gy, y_far, r2_hbm.at[0])]
    s += [second(1 + n, gy, t, r2_hbm.at[0]) for n, t in enumerate(others)]
    s += [second(8 + n, far_gy, t) for n, t in enumerate(others)]

    def late_at(c):
        return c * 2 * CHUNK

    def one(c):
        at = rows_at(c * SMALL, SMALL)
        return flow(AT_ONE + c, sent1.at[at], recv1.at[at], z_far)

    def two(c):
        target = late.at[rows_at(late_at(c) + CHUNK, SMALL)]
        return flow(AT_TWO + c, sent2.at[rows_at(c * SMALL, SMALL)], target, y_far)

    ranks = flow(AT_RANK, rank_out, rank_in, y_far)

    for name in list(f)[:6]:
        f[name].start()
    for n in range(1, 8):
        s[n].start()

    lane = iota((1, HALF), 1)

    def of_block(ref, b):
        return ref[rows_at(b * 128, 128), 0:1]

    loads[0].wait()
    rows[0:1, :] = i1[...].astype(F32)
    to_column(rows.at[0:1], col1)
    held1[...] = jnp.zeros_like(held1)
    loads[1].wait()
    rows[1:2, :] = i2[...].astype(F32)
    own2 = rows[1:2, :]
    key = over_rows(
        lambda b: jnp.where(
            of_block(col1, b) == own2,
            iota((128, HALF), 0) + (b * 128 + 1).astype(F32),
            0.0,
        )
    )
    order = key * HALF + lane
    rows[2:3, :] = order
    rows[4:5, :] = jnp.where(key > 0.0, key + (ROWS - 1.0), own2)
    to_column(rows.at[2:3], colk)

    forward("up_low", "up_low_2", "near_up")
    forward("down_high", "down_high_2")
    forward("near_high", "up_near", "down_near")
    forward("down_low", "near_down")
    s[0].start()

    order = rows[2:3, :]
    rank = over_rows(lambda b: ones_where(of_block(colk, b) < order))
    rank_out[...] = jnp.broadcast_to(rank, rank_out.shape)
    rows[3:4, :] = rank
    ranks.start()

    @pl.loop(0, HALF // 128)
    def _(b):
        here = iota((128, HALF), 0) + (b * 128).astype(F32)
        found = jnp.where(rows[3:4, :] == here, rows[4:5, :], 0.0)
        colg[rows_at(b * 128, 128), :] = jnp.broadcast_to(
            jnp.sum(found, axis=1, keepdims=True), (128, 128)
        )

    def spread(row, first):
        for p in range(HALF // CHUNK):
            start = p * 2 * CHUNK + first
            to[0:1, start : start + CHUNK] = row[:, p * CHUNK : (p + 1) * CHUNK]

    def find_first():
        own1 = rows[0:1, :]
        taken = over_rows(lambda b: ones_where(of_block(col2, b) == own1))
        spread(jnp.where(taken > 0.0, -1.0, own1), 0)

    def find_second():
        ranks.wait_recv()
        rows[2:3, :] = rank_in[0:1, :]
        to_column(rows.at[2:3], colk)
        lanes = iota((128, HALF), 1)
        spread(
            over_rows(
                lambda b: jnp.where(of_block(colk, b) == lanes, of_block(col2, b), 0.0)
            ),
            CHUNK,
        )

    def table(ref, column):
        high = jnp.floor(ref * (1 / 128))
        low = column - jnp.floor(column * (1 / 128)) * 128
        hot_high = ones_where(high == iota((ROWS // 128, HALF), 0)).astype(BF16)
        hot_low = ones_where(low == iota((HALF, 128), 1)).astype(BF16)
        return dot(hot_high, hot_low)

    def find_kept():
        count[...] = table(rows[0:1, :], col1[...]) + table(rows[1:2, :], col2[...])
        same = iota((128, 128), 0) == iota((128, 128), 1)

        @pl.loop(0, ROWS // 128)
        def _(b):
            found = jnp.sum(
                jnp.where(same, count[pl.ds(b, 1), :], 0.0), axis=1, keepdims=True
            )
            column = jnp.where(found > 0.0, 0.0, 1.0)
            keep[rows_at(b * 128, 128), :] = jnp.broadcast_to(column, (128, 128))

    loads[2].wait()

    def pick(column, dst, b):
        at = rows_at(b * 256, 256)
        hot = ones_where(column[at, 0:1] == iota((256, ROWS), 1)).astype(BF16)
        dst[at, :] = dot(hot, x[...]).astype(BF16)

    pick(col1, sent1, 0)
    pl.loop(0, 1)(lambda b: pick(colg, raw2, b))
    forward("up_low_2", "near_far")
    forward("up_near", "up_near_2")
    forward("down_near", "down_near_2")
    s[0].wait_recv()
    for n in range(8, 15):
        s[n].start()
    for name in ("up_high", "down_high_2", "up_near_2", "down_near_2"):
        f[name].wait_recv()
    for c in range(2):
        one(c).start()
    pick(col1, sent1, 1)
    one(2).start()
    pl.loop(1, 4)(lambda b: pick(colg, raw2, b))
    to_column(rows.at[1:2], col2)
    find_first()

    loads[3].wait()
    for name in ("near_low", "near_up", "near_down", "near_far"):
        f[name].wait_recv()

    def prepare(b):
        at = rows_at(b * 256, 256)
        raw2[at, :] = dot(raw2[at, :], r1[...]).astype(BF16)

    prepare(0)

    def place(low, high, begin=False):
        size = (high - low) * CHUNK
        source = z[low * CHUNK : high * CHUNK, :]
        target = to[0:1, low * CHUNK : high * CHUNK]

        def step(t):
            at = rows_at(t * BLOCK, BLOCK)
            hit = target == iota((BLOCK, size), 0) + (t * BLOCK).astype(F32)
            new = dot(ones_where(hit).astype(BF16), source)
            if begin:
                old = dot(y[at, :], r2[...]) * keep[at, 0:1]
                old = old.astype(BF16).astype(F32)
            else:
                old = acc[at, :].astype(F32)
            acc[at, :] = (old + new).astype(BF16)

        return step

    def rotate_block(src, by, dst, t, size=BLOCK):
        at = rows_at(t * size, size)
        dst[at, :] = dot(src[at, :], by[...]).astype(BF16)

    def pass_on(c):
        at = rows_at(c * SMALL, SMALL)
        came = dot(recv1[at, :], r1[...]).astype(BF16)
        held1[at, :] = came
        late[rows_at(late_at(c), SMALL), :] = came

        def choose(depth):
            hot = ones_where(colg[at, 0:1] - float(ROWS) == iota((SMALL, depth), 1))
            new = dot(hot.astype(BF16), held1[0:depth, :])
            sent2[at, :] = (raw2[at, :].astype(F32) + new).astype(BF16)

        low = 0
        for depth in (256, 512, HALF):

            @pl.when((c * SMALL >= low) & (c * SMALL < depth))
            def _():
                choose(depth)

            low = depth

    def rotated(low, high):
        for n in range(low, high):
            two(n).wait_recv()

    def rest(c):
        def at_step(k):
            return pl.when(c == k)

        def pairs(low, high):
            rotated(low, high)
            pl.loop(low, high)(lambda t: rotate_block(late, r2, z, t, 256))

        @at_step(0)
        def _():
            pl.loop(2, 3)(lambda b: pick(col1, sent1, b))
            pl.loop(0, 2)(lambda t: rotate_block(x, r1, y, t))
            pl.loop(1, 2)(prepare)

        @at_step(1)
        def _():
            find_kept()
            pl.loop(2, 4)(lambda t: rotate_block(x, r1, y, t))

        @at_step(2)
        def _():
            pl.loop(3, 4)(lambda b: pick(col1, sent1, b))
            pl.loop(2, 4)(prepare)
            find_second()

        @at_step(3)
        def _():
            loads[4].wait()
            for n in range(1, 15):
                s[n].wait_recv()
            pairs(0, 2)
            pl.loop(0, 1)(place(0, 4, True))

        @at_step(4)
        def _():
            pl.loop(1, 3)(place(0, 4, True))

        @at_step(5)
        def _():
            pl.loop(3, 4)(place(0, 4, True))
            pairs(2, 4)
            pl.loop(0, 1)(place(4, 8))

        @at_step(6)
        def _():
            pl.loop(1, 4)(place(4, 8))
            pairs(4, 5)
            pl.loop(0, 4)(place(8, 10))

        @at_step(7)
        def _():
            z[14 * CHUNK : 15 * CHUNK, :] = dot(
                late[14 * CHUNK : 15 * CHUNK, :], r2[...]
            ).astype(BF16)
            pairs(5, 7)
            pl.loop(0, 4)(place(10, 15))

    @pl.loop(0, STEPS)
    def _(c):
        one(c).wait_recv()

        @pl.when(c < STEPS - AHEAD)
        def _():
            one(c + AHEAD).start()

        pass_on(c)
        two(c).start()
        rest(c)

    to_ref[...] = jnp.broadcast_to(to[0:1, 15 * CHUNK :], to_ref.shape)
    rotated(7, 8)
    last_ref[...] = dot(late[15 * CHUNK :, :], r2[...]).astype(BF16)

    for name in f:
        f[name].wait_send()
    for n in range(N_SECOND):
        s[n].wait_send()
    ranks.wait_send()
    for c in range(STEPS):
        one(c).wait_send()
        two(c).wait_send()


def finish(acc, last, to, out_hbm, out, sem):
    def stored(t):
        at = rows_at(t * TAIL, TAIL)
        return pltpu.make_async_copy(out.at[at], out_hbm.at[at], sem.at[t])

    @pl.loop(0, ROWS // TAIL)
    def _(t):
        at = rows_at(t * TAIL, TAIL)
        hit = to[0:1, :] == iota((TAIL, CHUNK), 0) + (t * TAIL).astype(F32)
        new = dot(ones_where(hit).astype(BF16), last[...])
        out[at, :] = (acc[at, :].astype(F32) + new).astype(BF16)
        stored(t).start()

    for t in range(ROWS // TAIL):
        stored(t).wait()


def on_device(corpus, rotation_first, rotation_second, cross_first, cross_second):
    hbm = pl.BlockSpec(memory_space=pltpu.HBM)
    vmem = pl.BlockSpec(memory_space=pltpu.VMEM)
    acc, last, to = pl.pallas_call(
        kernel,
        out_shape=(
            jax.ShapeDtypeStruct((ROWS, D), BF16),
            jax.ShapeDtypeStruct((CHUNK, D), BF16),
            jax.ShapeDtypeStruct((8, CHUNK), F32),
        ),
        in_specs=[hbm] * 5,
        out_specs=(vmem, vmem, vmem),
        scratch_shapes=[
            pltpu.VMEM((ROWS, D), BF16),
            pltpu.VMEM((D, D), BF16),
            pltpu.VMEM((D, D), BF16),
            pltpu.VMEM((1, HALF), jnp.int32),
            pltpu.VMEM((1, HALF), jnp.int32),
            pltpu.VMEM((HALF, D), BF16),
            pltpu.VMEM((HALF, D), BF16),
            pltpu.VMEM((HALF, D), BF16),
            pltpu.VMEM((HALF, D), BF16),
            pltpu.VMEM((HALF, D), BF16),
            pltpu.VMEM((ROWS, D), BF16),
            pltpu.VMEM((ROWS, D), BF16),
            pltpu.VMEM((ROWS, D), BF16),
            pltpu.VMEM((HALF, 128), F32),
            pltpu.VMEM((HALF, 128), F32),
            pltpu.VMEM((HALF, 128), F32),
            pltpu.VMEM((HALF, 128), F32),
            pltpu.VMEM((ROWS, 128), F32),
            pltpu.VMEM((ROWS // 128, 128), F32),
            pltpu.VMEM((8, HALF), F32),
            pltpu.VMEM((8, ROWS), F32),
            pltpu.VMEM((8, HALF), F32),
            pltpu.VMEM((8, HALF), F32),
            pltpu.SemaphoreType.DMA((FLOWS,)),
            pltpu.SemaphoreType.DMA((FLOWS,)),
            pltpu.SemaphoreType.DMA((5,)),
        ],
        compiler_params=pltpu.CompilerParams(
            collective_id=0, has_side_effects=True, vmem_limit_bytes=VMEM
        ),
        cost_estimate=pl.CostEstimate(
            flops=36_000_000_000, bytes_accessed=16 << 20, transcendentals=0
        ),
    )(
        corpus,
        rotation_first,
        rotation_second,
        cross_first,
        cross_second,
    )
    return pl.pallas_call(
        finish,
        out_shape=jax.ShapeDtypeStruct((ROWS, D), BF16),
        in_specs=[vmem] * 3,
        out_specs=hbm,
        scratch_shapes=[
            pltpu.VMEM((ROWS, D), BF16),
            pltpu.SemaphoreType.DMA((ROWS // TAIL,)),
        ],
        compiler_params=pltpu.CompilerParams(vmem_limit_bytes=12 << 20),
        cost_estimate=pl.CostEstimate(
            flops=600_000_000, bytes_accessed=8 << 20, transcendentals=0
        ),
    )(acc, last, to)


def solution(mesh):
    in_specs = (
        P(("gx", "gy"), None),
        P("gy", "gx", None),
        P("gx", "gy", None),
        P("gx", "gy", None),
        P("gx", "gy", None),
    )
    out_specs = P(("gx", "gy"), None)
    return jax.shard_map(
        on_device, mesh=mesh, in_specs=in_specs, out_specs=out_specs, check_vma=False
    )
```

```python
import jax
import jax.numpy as jnp
from jax import lax
from jax.experimental import pallas as pl
from jax.experimental.pallas import tpu as pltpu
from jax.sharding import PartitionSpec as P

MESH = pl.DeviceIdType.MESH
F32, BF16 = jnp.float32, jnp.bfloat16

D = 1024
ROWS = 2048
HALF = 1024
CHUNK = 128
SMALL = 128
STEPS = HALF // SMALL
AHEAD = 3
FIRST = 128
SECOND = 64
N_FIRST, N_SECOND = 14, 15
BLOCK = 512
VMEM = 48 << 20
TAIL = 256

AT_SECOND = N_FIRST
AT_ONE = AT_SECOND + N_SECOND
AT_TWO = AT_ONE + STEPS
AT_RANK = AT_TWO + STEPS
FLOWS = AT_RANK + 1


def rows_at(start, size, unit=16):
    if isinstance(start, int):
        return pl.ds(start, size)
    return pl.ds(pl.multiple_of(start, unit), size)


def dot(a, b):
    return jnp.dot(a, b, preferred_element_type=F32)


def ones_where(mask):
    return jnp.where(mask, 1.0, 0.0)


def iota(shape, dim):
    return lax.broadcasted_iota(jnp.int32, shape, dim).astype(F32)


def to_column(row_ref, column_ref):
    same = iota((128, 128), 0) == iota((128, 128), 1)

    @pl.loop(0, HALF // 128)
    def _(b):
        piece = row_ref[0:1, pl.ds(pl.multiple_of(b * 128, 128), 128)]
        column = jnp.sum(jnp.where(same, piece, 0.0), axis=1, keepdims=True)
        column_ref[rows_at(b * 128, 128), :] = jnp.broadcast_to(column, (128, 128))


def over_rows(term):
    def step(b, total):
        return total + jnp.sum(term(b), axis=0, keepdims=True)

    return lax.fori_loop(0, HALF // 128, step, jnp.zeros((1, HALF), F32))


def kernel(
    x_hbm, r1_hbm, r2_hbm, i1_hbm, i2_hbm, acc, last_ref, to_ref,
    x, r1, r2, i1, i2, sent1, recv1, held1, raw2, sent2, y, late, z,
    col1, col2, colk, colg, keep, count, rows, to, rank_out, rank_in,
    send_sem, recv_sem, load_sem,
):
    gx, gy = lax.axis_index("gx"), lax.axis_index("gy")
    pz, py = gx // 2, gx % 2
    half, px, pc = gy // 8, (gy // 2) % 4, gy % 2

    def on_z(step):
        return lax.rem(pz + step + 4, 4)

    def part(zz, yy):
        return (zz * 2 + yy) * FIRST

    z_up, z_down, z_far = ((on_z(s) * 2 + py, gy) for s in (1, -1, 2))
    y_near = (pz * 2 + 1 - py, gy)
    far_gy = lax.rem(gy + 8, 16)
    y_far = (gx, far_gy)
    others = [
        (gx, half * 8 + lax.rem(px + dx, 4) * 2 + lax.rem(pc + dc, 2))
        for dx in range(4)
        for dc in range(2)
        if dx or dc
    ]

    loads = [
        pltpu.make_async_copy(src, dst, load_sem.at[i])
        for i, (src, dst) in enumerate(
            (
                (i1_hbm.at[0], i1),
                (i2_hbm.at[0], i2),
                (x_hbm, x),
                (r1_hbm.at[0], r1.at[rows_at(gx * FIRST, FIRST)]),
                (r2_hbm.at[0], r2.at[rows_at(gy * SECOND, SECOND)]),
            )
        )
    ]
    for load in loads:
        load.start()

    barrier = pltpu.get_barrier_semaphore()
    partners = [z_up, z_down, z_far, y_near, y_far, *others]
    for partner in partners:
        pl.semaphore_signal(barrier, inc=1, device_id=partner, device_id_type=MESH)
    pl.semaphore_wait(barrier, len(partners))

    def flow(number, src, dst, target):
        return pltpu.make_async_remote_copy(
            src_ref=src,
            dst_ref=dst,
            send_sem=send_sem.at[number],
            recv_sem=recv_sem.at[number],
            device_id=target,
            device_id_type=MESH,
        )

    def first(number, zz, yy, low, size, target, src=None):
        there = r1.at[rows_at(part(zz, yy) + low, size)]
        return flow(number, there if src is None else src, there, target)

    low, high = 0, FIRST // 2
    f = {
        "up_low": first(0, pz, py, low, 64, z_up, r1_hbm.at[0, 0:64]),
        "down_high": first(1, pz, py, high, 64, z_down, r1_hbm.at[0, 64:128]),
        "near_high": first(2, pz, py, high, 64, y_near, r1_hbm.at[0, 64:128]),
        "up_high": first(3, pz, py, high, 64, z_up, r1_hbm.at[0, 64:128]),
        "down_low": first(4, pz, py, low, 64, z_down, r1_hbm.at[0, 0:64]),
        "near_low": first(5, pz, py, low, 64, y_near, r1_hbm.at[0, 0:64]),
        "up_low_2": first(6, on_z(-1), py, low, 64, z_up),
        "down_high_2": first(7, on_z(1), py, high, 64, z_down),
        "near_up": first(8, on_z(-1), py, low, 64, y_near),
        "near_down": first(9, on_z(1), py, low, 64, y_near),
        "up_near": first(10, pz, 1 - py, high, 64, z_up),
        "down_near": first(11, pz, 1 - py, high, 64, z_down),
        "near_far": first(12, on_z(2), py, low, 64, y_near),
        "near_far_high": first(13, on_z(2), py, high, 64, y_near),
    }

    def forward(came, *names):
        f[came].wait_recv()
        for name in names:
            f[name].start()

    def second(number, owner, target, src=None):
        there = r2.at[rows_at(owner * SECOND, SECOND)]
        return flow(AT_SECOND + number, there if src is None else src, there, target)

    s = [second(0, gy, y_far, r2_hbm.at[0])]
    s += [second(1 + n, gy, t, r2_hbm.at[0]) for n, t in enumerate(others)]
    s += [second(8 + n, far_gy, t) for n, t in enumerate(others)]

    def late_at(c):
        return c * 2 * CHUNK

    def one(c):
        at = rows_at(c * SMALL, SMALL)
        return flow(AT_ONE + c, sent1.at[at], recv1.at[at], z_far)

    def two(c):
        target = late.at[rows_at(late_at(c) + CHUNK, SMALL)]
        return flow(AT_TWO + c, sent2.at[rows_at(c * SMALL, SMALL)], target, y_far)

    ranks = flow(AT_RANK, rank_out, rank_in, y_far)

    for name in list(f)[:6]:
        f[name].start()
    for n in range(1, 8):
        s[n].start()

    lane = iota((1, HALF), 1)

    def of_block(ref, b):
        return ref[rows_at(b * 128, 128), 0:1]

    loads[0].wait()
    rows[0:1, :] = i1[...].astype(F32)
    to_column(rows.at[0:1], col1)
    held1[...] = jnp.zeros_like(held1)
    loads[1].wait()
    rows[1:2, :] = i2[...].astype(F32)
    own2 = rows[1:2, :]
    key = over_rows(
        lambda b: jnp.where(
            of_block(col1, b) == own2,
            iota((128, HALF), 0) + (b * 128 + 1).astype(F32),
            0.0,
        )
    )
    order = key * HALF + lane
    rows[2:3, :] = order
    rows[4:5, :] = jnp.where(key > 0.0, key + (ROWS - 1.0), own2)
    to_column(rows.at[2:3], colk)

    forward("up_low", "up_low_2", "near_up")
    forward("down_high", "down_high_2")
    forward("near_high", "up_near", "down_near")
    forward("down_low", "near_down")
    s[0].start()

    order = rows[2:3, :]
    rank = over_rows(lambda b: ones_where(of_block(colk, b) < order))
    rank_out[...] = jnp.broadcast_to(rank, rank_out.shape)
    rows[3:4, :] = rank
    ranks.start()

    @pl.loop(0, HALF // 128)
    def _(b):
        here = iota((128, HALF), 0) + (b * 128).astype(F32)
        found = jnp.where(rows[3:4, :] == here, rows[4:5, :], 0.0)
        colg[rows_at(b * 128, 128), :] = jnp.broadcast_to(
            jnp.sum(found, axis=1, keepdims=True), (128, 128)
        )

    def spread(row, first):
        for p in range(HALF // CHUNK):
            start = p * 2 * CHUNK + first
            to[0:1, start : start + CHUNK] = row[:, p * CHUNK : (p + 1) * CHUNK]

    def find_first():
        own1 = rows[0:1, :]
        taken = over_rows(lambda b: ones_where(of_block(col2, b) == own1))
        spread(jnp.where(taken > 0.0, -1.0, own1), 0)

    def find_second():
        ranks.wait_recv()
        rows[2:3, :] = rank_in[0:1, :]
        to_column(rows.at[2:3], colk)
        lanes = iota((128, HALF), 1)
        spread(
            over_rows(
                lambda b: jnp.where(of_block(colk, b) == lanes, of_block(col2, b), 0.0)
            ),
            CHUNK,
        )

    def table(ref, column):
        high = jnp.floor(ref * (1 / 128))
        low = column - jnp.floor(column * (1 / 128)) * 128
        hot_high = ones_where(high == iota((ROWS // 128, HALF), 0)).astype(BF16)
        hot_low = ones_where(low == iota((HALF, 128), 1)).astype(BF16)
        return dot(hot_high, hot_low)

    def find_kept():
        count[...] = table(rows[0:1, :], col1[...]) + table(rows[1:2, :], col2[...])
        same = iota((128, 128), 0) == iota((128, 128), 1)

        @pl.loop(0, ROWS // 128)
        def _(b):
            found = jnp.sum(
                jnp.where(same, count[pl.ds(b, 1), :], 0.0), axis=1, keepdims=True
            )
            column = jnp.where(found > 0.0, 0.0, 1.0)
            keep[rows_at(b * 128, 128), :] = jnp.broadcast_to(column, (128, 128))

    loads[2].wait()

    def pick(column, dst, b):
        at = rows_at(b * 256, 256)
        hot = ones_where(column[at, 0:1] == iota((256, ROWS), 1)).astype(BF16)
        dst[at, :] = dot(hot, x[...]).astype(BF16)

    pick(col1, sent1, 0)
    pl.loop(0, 1)(lambda b: pick(colg, raw2, b))
    forward("up_low_2", "near_far")
    forward("down_high_2", "near_far_high")
    for name in ("up_high", "up_near", "down_near"):
        f[name].wait_recv()
    for c in range(2):
        one(c).start()
    pick(col1, sent1, 1)
    one(2).start()
    pl.loop(1, 4)(lambda b: pick(colg, raw2, b))
    to_column(rows.at[1:2], col2)
    find_first()

    loads[3].wait()
    for name in ("near_low", "near_up", "near_down", "near_far", "near_far_high"):
        f[name].wait_recv()

    s[0].wait_recv()
    for n in range(8, 15):
        s[n].start()

    def prepare(b):
        at = rows_at(b * 256, 256)
        raw2[at, :] = dot(raw2[at, :], r1[...]).astype(BF16)

    prepare(0)

    def place(low, high, begin=False):
        size = (high - low) * CHUNK
        source = z[low * CHUNK : high * CHUNK, :]
        target = to[0:1, low * CHUNK : high * CHUNK]

        def step(t):
            at = rows_at(t * BLOCK, BLOCK)
            hit = target == iota((BLOCK, size), 0) + (t * BLOCK).astype(F32)
            new = dot(ones_where(hit).astype(BF16), source)
            if begin:
                old = dot(y[at, :], r2[...]) * keep[at, 0:1]
                old = old.astype(BF16).astype(F32)
            else:
                old = acc[at, :].astype(F32)
            acc[at, :] = (old + new).astype(BF16)

        return step

    def rotate_block(src, by, dst, t, size=BLOCK):
        at = rows_at(t * size, size)
        dst[at, :] = dot(src[at, :], by[...]).astype(BF16)

    def pass_on(c):
        at = rows_at(c * SMALL, SMALL)
        came = dot(recv1[at, :], r1[...]).astype(BF16)
        held1[at, :] = came
        late[rows_at(late_at(c), SMALL), :] = came

        def choose(depth):
            hot = ones_where(colg[at, 0:1] - float(ROWS) == iota((SMALL, depth), 1))
            new = dot(hot.astype(BF16), held1[0:depth, :])
            sent2[at, :] = (raw2[at, :].astype(F32) + new).astype(BF16)

        low = 0
        for depth in (256, 512, HALF):

            @pl.when((c * SMALL >= low) & (c * SMALL < depth))
            def _():
                choose(depth)

            low = depth

    def rotated(low, high):
        for n in range(low, high):
            two(n).wait_recv()

    def rest(c):
        def at_step(k):
            return pl.when(c == k)

        def pairs(low, high):
            rotated(low, high)
            pl.loop(low, high)(lambda t: rotate_block(late, r2, z, t, 256))

        @at_step(0)
        def _():
            pl.loop(2, 3)(lambda b: pick(col1, sent1, b))
            pl.loop(0, 2)(lambda t: rotate_block(x, r1, y, t))
            pl.loop(1, 2)(prepare)

        @at_step(1)
        def _():
            find_kept()
            pl.loop(2, 4)(lambda t: rotate_block(x, r1, y, t))

        @at_step(2)
        def _():
            pl.loop(3, 4)(lambda b: pick(col1, sent1, b))
            pl.loop(2, 4)(prepare)
            find_second()

        @at_step(3)
        def _():
            loads[4].wait()
            for n in range(1, 15):
                s[n].wait_recv()
            pairs(0, 2)
            pl.loop(0, 1)(place(0, 4, True))

        @at_step(4)
        def _():
            pl.loop(1, 3)(place(0, 4, True))

        @at_step(5)
        def _():
            pl.loop(3, 4)(place(0, 4, True))
            pairs(2, 4)
            pl.loop(0, 1)(place(4, 8))

        @at_step(6)
        def _():
            pl.loop(1, 4)(place(4, 8))
            pairs(4, 5)
            pl.loop(0, 4)(place(8, 10))

        @at_step(7)
        def _():
            z[14 * CHUNK : 15 * CHUNK, :] = dot(
                late[14 * CHUNK : 15 * CHUNK, :], r2[...]
            ).astype(BF16)
            pairs(5, 7)
            pl.loop(0, 4)(place(10, 15))

    @pl.loop(0, STEPS)
    def _(c):
        one(c).wait_recv()

        @pl.when(c < STEPS - AHEAD)
        def _():
            one(c + AHEAD).start()

        pass_on(c)
        two(c).start()
        rest(c)

    to_ref[...] = jnp.broadcast_to(to[0:1, 15 * CHUNK :], to_ref.shape)
    rotated(7, 8)
    last_ref[...] = dot(late[15 * CHUNK :, :], r2[...]).astype(BF16)

    for name in f:
        f[name].wait_send()
    for n in range(N_SECOND):
        s[n].wait_send()
    ranks.wait_send()
    for c in range(STEPS):
        one(c).wait_send()
        two(c).wait_send()


def finish(acc, last, to, out_hbm, out, sem):
    def stored(t):
        at = rows_at(t * TAIL, TAIL)
        return pltpu.make_async_copy(out.at[at], out_hbm.at[at], sem.at[t])

    @pl.loop(0, ROWS // TAIL)
    def _(t):
        at = rows_at(t * TAIL, TAIL)
        hit = to[0:1, :] == iota((TAIL, CHUNK), 0) + (t * TAIL).astype(F32)
        new = dot(ones_where(hit).astype(BF16), last[...])
        out[at, :] = (acc[at, :].astype(F32) + new).astype(BF16)
        stored(t).start()

    for t in range(ROWS // TAIL):
        stored(t).wait()


def on_device(corpus, rotation_first, rotation_second, cross_first, cross_second):
    hbm = pl.BlockSpec(memory_space=pltpu.HBM)
    vmem = pl.BlockSpec(memory_space=pltpu.VMEM)
    acc, last, to = pl.pallas_call(
        kernel,
        out_shape=(
            jax.ShapeDtypeStruct((ROWS, D), BF16),
            jax.ShapeDtypeStruct((CHUNK, D), BF16),
            jax.ShapeDtypeStruct((8, CHUNK), F32),
        ),
        in_specs=[hbm] * 5,
        out_specs=(vmem, vmem, vmem),
        scratch_shapes=[
            pltpu.VMEM((ROWS, D), BF16),
            pltpu.VMEM((D, D), BF16),
            pltpu.VMEM((D, D), BF16),
            pltpu.VMEM((1, HALF), jnp.int32),
            pltpu.VMEM((1, HALF), jnp.int32),
            pltpu.VMEM((HALF, D), BF16),
            pltpu.VMEM((HALF, D), BF16),
            pltpu.VMEM((HALF, D), BF16),
            pltpu.VMEM((HALF, D), BF16),
            pltpu.VMEM((HALF, D), BF16),
            pltpu.VMEM((ROWS, D), BF16),
            pltpu.VMEM((ROWS, D), BF16),
            pltpu.VMEM((ROWS, D), BF16),
            pltpu.VMEM((HALF, 128), F32),
            pltpu.VMEM((HALF, 128), F32),
            pltpu.VMEM((HALF, 128), F32),
            pltpu.VMEM((HALF, 128), F32),
            pltpu.VMEM((ROWS, 128), F32),
            pltpu.VMEM((ROWS // 128, 128), F32),
            pltpu.VMEM((8, HALF), F32),
            pltpu.VMEM((8, ROWS), F32),
            pltpu.VMEM((8, HALF), F32),
            pltpu.VMEM((8, HALF), F32),
            pltpu.SemaphoreType.DMA((FLOWS,)),
            pltpu.SemaphoreType.DMA((FLOWS,)),
            pltpu.SemaphoreType.DMA((5,)),
        ],
        compiler_params=pltpu.CompilerParams(
            collective_id=0, has_side_effects=True, vmem_limit_bytes=VMEM
        ),
        cost_estimate=pl.CostEstimate(
            flops=36_000_000_000, bytes_accessed=16 << 20, transcendentals=0
        ),
    )(
        corpus,
        rotation_first,
        rotation_second,
        cross_first,
        cross_second,
    )
    return pl.pallas_call(
        finish,
        out_shape=jax.ShapeDtypeStruct((ROWS, D), BF16),
        in_specs=[vmem] * 3,
        out_specs=hbm,
        scratch_shapes=[
            pltpu.VMEM((ROWS, D), BF16),
            pltpu.SemaphoreType.DMA((ROWS // TAIL,)),
        ],
        compiler_params=pltpu.CompilerParams(vmem_limit_bytes=12 << 20),
        cost_estimate=pl.CostEstimate(
            flops=600_000_000, bytes_accessed=8 << 20, transcendentals=0
        ),
    )(acc, last, to)


def solution(mesh):
    in_specs = (
        P(("gx", "gy"), None),
        P("gy", "gx", None),
        P("gx", "gy", None),
        P("gx", "gy", None),
        P("gx", "gy", None),
    )
    out_specs = P(("gx", "gy"), None)
    return jax.shard_map(
        on_device, mesh=mesh, in_specs=in_specs, out_specs=out_specs, check_vma=False
    )
```

```python
import jax
import jax.numpy as jnp
from jax import lax
from jax.experimental import pallas as pl
from jax.experimental.pallas import tpu as pltpu
from jax.sharding import PartitionSpec as P

MESH = pl.DeviceIdType.MESH
F32, BF16 = jnp.float32, jnp.bfloat16

D = 1024
ROWS = 2048
HALF = 1024
CHUNK = 128
SMALL = 128
STEPS = HALF // SMALL
AHEAD = 3
FIRST = 128
SECOND = 64
N_FIRST, N_SECOND = 14, 15
BLOCK = 512
VMEM = 48 << 20
TAIL = 512

AT_SECOND = N_FIRST
AT_ONE = AT_SECOND + N_SECOND
AT_TWO = AT_ONE + STEPS
AT_RANK = AT_TWO + STEPS
FLOWS = AT_RANK + 1


def rows_at(start, size, unit=16):
    if isinstance(start, int):
        return pl.ds(start, size)
    return pl.ds(pl.multiple_of(start, unit), size)


def dot(a, b):
    return jnp.dot(a, b, preferred_element_type=F32)


def ones_where(mask):
    return jnp.where(mask, 1.0, 0.0)


def iota(shape, dim):
    return lax.broadcasted_iota(jnp.int32, shape, dim).astype(F32)


def to_column(row_ref, column_ref):
    same = iota((128, 128), 0) == iota((128, 128), 1)

    @pl.loop(0, HALF // 128)
    def _(b):
        piece = row_ref[0:1, pl.ds(pl.multiple_of(b * 128, 128), 128)]
        column = jnp.sum(jnp.where(same, piece, 0.0), axis=1, keepdims=True)
        column_ref[rows_at(b * 128, 128), :] = jnp.broadcast_to(column, (128, 128))


def over_rows(term):
    def step(b, total):
        return total + jnp.sum(term(b), axis=0, keepdims=True)

    return lax.fori_loop(0, HALF // 128, step, jnp.zeros((1, HALF), F32))


def kernel(
    x_hbm, r1_hbm, r2_hbm, i1_hbm, i2_hbm, acc, last_ref, to_ref,
    x, r1, r2, i1, i2, sent1, recv1, held1, raw2, sent2, y, late, z,
    col1, col2, colk, colg, keep, count, rows, to, rank_out, rank_in,
    send_sem, recv_sem, load_sem,
):
    gx, gy = lax.axis_index("gx"), lax.axis_index("gy")
    pz, py = gx // 2, gx % 2
    half, px, pc = gy // 8, (gy // 2) % 4, gy % 2

    def on_z(step):
        return lax.rem(pz + step + 4, 4)

    def part(zz, yy):
        return (zz * 2 + yy) * FIRST

    z_up, z_down, z_far = ((on_z(s) * 2 + py, gy) for s in (1, -1, 2))
    y_near = (pz * 2 + 1 - py, gy)
    far_gy = lax.rem(gy + 8, 16)
    y_far = (gx, far_gy)
    others = [
        (gx, half * 8 + lax.rem(px + dx, 4) * 2 + lax.rem(pc + dc, 2))
        for dx in range(4)
        for dc in range(2)
        if dx or dc
    ]

    loads = [
        pltpu.make_async_copy(src, dst, load_sem.at[i])
        for i, (src, dst) in enumerate(
            (
                (i1_hbm.at[0], i1),
                (i2_hbm.at[0], i2),
                (x_hbm, x),
                (r1_hbm.at[0], r1.at[rows_at(gx * FIRST, FIRST)]),
                (r2_hbm.at[0], r2.at[rows_at(gy * SECOND, SECOND)]),
            )
        )
    ]
    for load in loads:
        load.start()

    barrier = pltpu.get_barrier_semaphore()
    partners = [z_up, z_down, z_far, y_near, y_far, *others]
    for partner in partners:
        pl.semaphore_signal(barrier, inc=1, device_id=partner, device_id_type=MESH)
    pl.semaphore_wait(barrier, len(partners))

    def flow(number, src, dst, target):
        return pltpu.make_async_remote_copy(
            src_ref=src,
            dst_ref=dst,
            send_sem=send_sem.at[number],
            recv_sem=recv_sem.at[number],
            device_id=target,
            device_id_type=MESH,
        )

    def first(number, zz, yy, low, size, target, src=None):
        there = r1.at[rows_at(part(zz, yy) + low, size)]
        return flow(number, there if src is None else src, there, target)

    low, high = 0, FIRST // 2
    f = {
        "up_low": first(0, pz, py, low, 64, z_up, r1_hbm.at[0, 0:64]),
        "down_high": first(1, pz, py, high, 64, z_down, r1_hbm.at[0, 64:128]),
        "near_high": first(2, pz, py, high, 64, y_near, r1_hbm.at[0, 64:128]),
        "up_high": first(3, pz, py, high, 64, z_up, r1_hbm.at[0, 64:128]),
        "down_low": first(4, pz, py, low, 64, z_down, r1_hbm.at[0, 0:64]),
        "near_low": first(5, pz, py, low, 64, y_near, r1_hbm.at[0, 0:64]),
        "up_low_2": first(6, on_z(-1), py, low, 64, z_up),
        "down_high_2": first(7, on_z(1), py, high, 64, z_down),
        "near_up": first(8, on_z(-1), py, low, 64, y_near),
        "near_down": first(9, on_z(1), py, low, 64, y_near),
        "up_near": first(10, pz, 1 - py, high, 64, z_up),
        "down_near": first(11, pz, 1 - py, high, 64, z_down),
        "near_far": first(12, on_z(2), py, low, 64, y_near),
        "near_far_high": first(13, on_z(2), py, high, 64, y_near),
    }

    def forward(came, *names):
        f[came].wait_recv()
        for name in names:
            f[name].start()

    def second(number, owner, target, src=None):
        there = r2.at[rows_at(owner * SECOND, SECOND)]
        return flow(AT_SECOND + number, there if src is None else src, there, target)

    s = [second(0, gy, y_far, r2_hbm.at[0])]
    s += [second(1 + n, gy, t, r2_hbm.at[0]) for n, t in enumerate(others)]
    s += [second(8 + n, far_gy, t) for n, t in enumerate(others)]

    def late_at(c):
        return c * 2 * CHUNK

    def one(c):
        at = rows_at(c * SMALL, SMALL)
        return flow(AT_ONE + c, sent1.at[at], recv1.at[at], z_far)

    def two(c):
        target = late.at[rows_at(late_at(c) + CHUNK, SMALL)]
        return flow(AT_TWO + c, sent2.at[rows_at(c * SMALL, SMALL)], target, y_far)

    ranks = flow(AT_RANK, rank_out, rank_in, y_far)

    for name in list(f)[:6]:
        f[name].start()
    for n in range(1, 8):
        s[n].start()

    lane = iota((1, HALF), 1)

    def of_block(ref, b):
        return ref[rows_at(b * 128, 128), 0:1]

    loads[0].wait()
    rows[0:1, :] = i1[...].astype(F32)
    to_column(rows.at[0:1], col1)
    held1[...] = jnp.zeros_like(held1)
    loads[1].wait()
    rows[1:2, :] = i2[...].astype(F32)
    own2 = rows[1:2, :]
    key = over_rows(
        lambda b: jnp.where(
            of_block(col1, b) == own2,
            iota((128, HALF), 0) + (b * 128 + 1).astype(F32),
            0.0,
        )
    )
    order = key * HALF + lane
    rows[2:3, :] = order
    rows[4:5, :] = jnp.where(key > 0.0, key + (ROWS - 1.0), own2)
    to_column(rows.at[2:3], colk)

    forward("up_low", "up_low_2", "near_up")
    forward("down_high", "down_high_2")
    forward("near_high", "up_near", "down_near")
    forward("down_low", "near_down")
    s[0].start()

    order = rows[2:3, :]
    rank = over_rows(lambda b: ones_where(of_block(colk, b) < order))
    rank_out[...] = jnp.broadcast_to(rank, rank_out.shape)
    rows[3:4, :] = rank
    ranks.start()

    @pl.loop(0, HALF // 128)
    def _(b):
        here = iota((128, HALF), 0) + (b * 128).astype(F32)
        found = jnp.where(rows[3:4, :] == here, rows[4:5, :], 0.0)
        colg[rows_at(b * 128, 128), :] = jnp.broadcast_to(
            jnp.sum(found, axis=1, keepdims=True), (128, 128)
        )

    def spread(row, first):
        for p in range(HALF // CHUNK):
            start = p * 2 * CHUNK + first
            to[0:1, start : start + CHUNK] = row[:, p * CHUNK : (p + 1) * CHUNK]

    def find_first():
        own1 = rows[0:1, :]
        taken = over_rows(lambda b: ones_where(of_block(col2, b) == own1))
        spread(jnp.where(taken > 0.0, -1.0, own1), 0)

    def find_second():
        ranks.wait_recv()
        rows[2:3, :] = rank_in[0:1, :]
        to_column(rows.at[2:3], colk)
        lanes = iota((128, HALF), 1)
        spread(
            over_rows(
                lambda b: jnp.where(of_block(colk, b) == lanes, of_block(col2, b), 0.0)
            ),
            CHUNK,
        )

    def table(ref, column):
        high = jnp.floor(ref * (1 / 128))
        low = column - jnp.floor(column * (1 / 128)) * 128
        hot_high = ones_where(high == iota((ROWS // 128, HALF), 0)).astype(BF16)
        hot_low = ones_where(low == iota((HALF, 128), 1)).astype(BF16)
        return dot(hot_high, hot_low)

    def find_kept():
        count[...] = table(rows[0:1, :], col1[...]) + table(rows[1:2, :], col2[...])
        same = iota((128, 128), 0) == iota((128, 128), 1)

        @pl.loop(0, ROWS // 128)
        def _(b):
            found = jnp.sum(
                jnp.where(same, count[pl.ds(b, 1), :], 0.0), axis=1, keepdims=True
            )
            column = jnp.where(found > 0.0, 0.0, 1.0)
            keep[rows_at(b * 128, 128), :] = jnp.broadcast_to(column, (128, 128))

    loads[2].wait()

    def pick(column, dst, b):
        at = rows_at(b * 256, 256)
        hot = ones_where(column[at, 0:1] == iota((256, ROWS), 1)).astype(BF16)
        dst[at, :] = dot(hot, x[...]).astype(BF16)

    pick(col1, sent1, 0)
    pl.loop(0, 1)(lambda b: pick(colg, raw2, b))
    forward("up_low_2", "near_far")
    forward("down_high_2", "near_far_high")
    for name in ("up_high", "up_near", "down_near"):
        f[name].wait_recv()
    for c in range(2):
        one(c).start()
    pick(col1, sent1, 1)
    one(2).start()
    pl.loop(1, 4)(lambda b: pick(colg, raw2, b))
    to_column(rows.at[1:2], col2)
    find_first()

    loads[3].wait()
    for name in ("near_low", "near_up", "near_down", "near_far", "near_far_high"):
        f[name].wait_recv()

    s[0].wait_recv()
    for n in range(8, 15):
        s[n].start()

    def prepare(b):
        at = rows_at(b * 256, 256)
        raw2[at, :] = dot(raw2[at, :], r1[...]).astype(BF16)

    prepare(0)

    def place(low, high, begin=False):
        size = (high - low) * CHUNK
        source = z[low * CHUNK : high * CHUNK, :]
        target = to[0:1, low * CHUNK : high * CHUNK]

        def step(t):
            at = rows_at(t * BLOCK, BLOCK)
            hit = target == iota((BLOCK, size), 0) + (t * BLOCK).astype(F32)
            new = dot(ones_where(hit).astype(BF16), source)
            if begin:
                old = dot(y[at, :], r2[...]) * keep[at, 0:1]
                old = old.astype(BF16).astype(F32)
            else:
                old = acc[at, :].astype(F32)
            acc[at, :] = (old + new).astype(BF16)

        return step

    def rotate_block(src, by, dst, t, size=BLOCK):
        at = rows_at(t * size, size)
        dst[at, :] = dot(src[at, :], by[...]).astype(BF16)

    def pass_on(c):
        at = rows_at(c * SMALL, SMALL)
        came = dot(recv1[at, :], r1[...]).astype(BF16)
        held1[at, :] = came
        late[rows_at(late_at(c), SMALL), :] = came

        def choose(depth):
            hot = ones_where(colg[at, 0:1] - float(ROWS) == iota((SMALL, depth), 1))
            new = dot(hot.astype(BF16), held1[0:depth, :])
            sent2[at, :] = (raw2[at, :].astype(F32) + new).astype(BF16)

        low = 0
        for depth in (256, 512, HALF):

            @pl.when((c * SMALL >= low) & (c * SMALL < depth))
            def _():
                choose(depth)

            low = depth

    def rotated(low, high):
        for n in range(low, high):
            two(n).wait_recv()

    def rest(c):
        def at_step(k):
            return pl.when(c == k)

        def pairs(low, high):
            rotated(low, high)
            pl.loop(low, high)(lambda t: rotate_block(late, r2, z, t, 256))

        @at_step(0)
        def _():
            pl.loop(2, 3)(lambda b: pick(col1, sent1, b))
            pl.loop(0, 2)(lambda t: rotate_block(x, r1, y, t))
            pl.loop(1, 2)(prepare)

        @at_step(1)
        def _():
            find_kept()
            pl.loop(2, 4)(lambda t: rotate_block(x, r1, y, t))

        @at_step(2)
        def _():
            pl.loop(3, 4)(lambda b: pick(col1, sent1, b))
            pl.loop(2, 4)(prepare)
            find_second()

        @at_step(3)
        def _():
            loads[4].wait()
            for n in range(1, 15):
                s[n].wait_recv()
            pairs(0, 2)
            pl.loop(0, 1)(place(0, 4, True))

        @at_step(4)
        def _():
            pl.loop(1, 3)(place(0, 4, True))

        @at_step(5)
        def _():
            pl.loop(3, 4)(place(0, 4, True))
            pairs(2, 4)
            pl.loop(0, 1)(place(4, 8))

        @at_step(6)
        def _():
            pl.loop(1, 4)(place(4, 8))
            pairs(4, 5)
            pl.loop(0, 4)(place(8, 10))

        @at_step(7)
        def _():
            z[14 * CHUNK : 15 * CHUNK, :] = dot(
                late[14 * CHUNK : 15 * CHUNK, :], r2[...]
            ).astype(BF16)
            pairs(5, 7)
            pl.loop(0, 4)(place(10, 15))

    @pl.loop(0, STEPS)
    def _(c):
        one(c).wait_recv()

        @pl.when(c < STEPS - AHEAD)
        def _():
            one(c + AHEAD).start()

        pass_on(c)
        two(c).start()
        rest(c)

    to_ref[...] = jnp.broadcast_to(to[0:1, 15 * CHUNK :], to_ref.shape)
    rotated(7, 8)
    last_ref[...] = dot(late[15 * CHUNK :, :], r2[...]).astype(BF16)

    for name in f:
        f[name].wait_send()
    for n in range(N_SECOND):
        s[n].wait_send()
    ranks.wait_send()
    for c in range(STEPS):
        one(c).wait_send()
        two(c).wait_send()


def finish(acc, last, to, out_hbm, out, sem):
    def stored(t):
        at = rows_at(t * TAIL, TAIL)
        return pltpu.make_async_copy(out.at[at], out_hbm.at[at], sem.at[t])

    @pl.loop(0, ROWS // TAIL)
    def _(t):
        at = rows_at(t * TAIL, TAIL)
        hit = to[0:1, :] == iota((TAIL, CHUNK), 0) + (t * TAIL).astype(F32)
        new = dot(ones_where(hit).astype(BF16), last[...])
        out[at, :] = (acc[at, :].astype(F32) + new).astype(BF16)
        stored(t).start()

    for t in range(ROWS // TAIL):
        stored(t).wait()


def on_device(corpus, rotation_first, rotation_second, cross_first, cross_second):
    hbm = pl.BlockSpec(memory_space=pltpu.HBM)
    vmem = pl.BlockSpec(memory_space=pltpu.VMEM)
    acc, last, to = pl.pallas_call(
        kernel,
        out_shape=(
            jax.ShapeDtypeStruct((ROWS, D), BF16),
            jax.ShapeDtypeStruct((CHUNK, D), BF16),
            jax.ShapeDtypeStruct((8, CHUNK), F32),
        ),
        in_specs=[hbm] * 5,
        out_specs=(vmem, vmem, vmem),
        scratch_shapes=[
            pltpu.VMEM((ROWS, D), BF16),
            pltpu.VMEM((D, D), BF16),
            pltpu.VMEM((D, D), BF16),
            pltpu.VMEM((1, HALF), jnp.int32),
            pltpu.VMEM((1, HALF), jnp.int32),
            pltpu.VMEM((HALF, D), BF16),
            pltpu.VMEM((HALF, D), BF16),
            pltpu.VMEM((HALF, D), BF16),
            pltpu.VMEM((HALF, D), BF16),
            pltpu.VMEM((HALF, D), BF16),
            pltpu.VMEM((ROWS, D), BF16),
            pltpu.VMEM((ROWS, D), BF16),
            pltpu.VMEM((ROWS, D), BF16),
            pltpu.VMEM((HALF, 128), F32),
            pltpu.VMEM((HALF, 128), F32),
            pltpu.VMEM((HALF, 128), F32),
            pltpu.VMEM((HALF, 128), F32),
            pltpu.VMEM((ROWS, 128), F32),
            pltpu.VMEM((ROWS // 128, 128), F32),
            pltpu.VMEM((8, HALF), F32),
            pltpu.VMEM((8, ROWS), F32),
            pltpu.VMEM((8, HALF), F32),
            pltpu.VMEM((8, HALF), F32),
            pltpu.SemaphoreType.DMA((FLOWS,)),
            pltpu.SemaphoreType.DMA((FLOWS,)),
            pltpu.SemaphoreType.DMA((5,)),
        ],
        compiler_params=pltpu.CompilerParams(
            collective_id=0, has_side_effects=True, vmem_limit_bytes=VMEM
        ),
        cost_estimate=pl.CostEstimate(
            flops=36_000_000_000, bytes_accessed=16 << 20, transcendentals=0
        ),
    )(
        corpus,
        rotation_first,
        rotation_second,
        cross_first,
        cross_second,
    )
    return pl.pallas_call(
        finish,
        out_shape=jax.ShapeDtypeStruct((ROWS, D), BF16),
        in_specs=[vmem] * 3,
        out_specs=hbm,
        scratch_shapes=[
            pltpu.VMEM((ROWS, D), BF16),
            pltpu.SemaphoreType.DMA((ROWS // TAIL,)),
        ],
        compiler_params=pltpu.CompilerParams(vmem_limit_bytes=12 << 20),
        cost_estimate=pl.CostEstimate(
            flops=600_000_000, bytes_accessed=8 << 20, transcendentals=0
        ),
    )(acc, last, to)


def solution(mesh):
    in_specs = (
        P(("gx", "gy"), None),
        P("gy", "gx", None),
        P("gx", "gy", None),
        P("gx", "gy", None),
        P("gx", "gy", None),
    )
    out_specs = P(("gx", "gy"), None)
    return jax.shard_map(
        on_device, mesh=mesh, in_specs=in_specs, out_specs=out_specs, check_vma=False
    )
```
